1024 devices in a mesh: expert: 64 (over y, z), hidden: 16 (over x, core).
Axes of the slice: x: 8, y: 8, z: 8, core: 2. Of those that a mesh axis runs over, the one named last changes fastest.
Arguments:
- tokens: bfloat16 [1024, 4096], P('expert', 'hidden'), may hold values from -6 to 6
- probs: float32 [1024, 8], P('expert'), may hold values from 0.05 to 0.6
- expert_ids: int32 [1024, 8], P('expert'), may hold values from 0 to 63, all different within a row; in each aligned block of 16 rows (0 to 15, 16 to 31, ...) at most 4 rows name the same one
- gate_weight: bfloat16 [64, 2048, 4096], P('expert', 'hidden'), may hold values from -0.09375 to 0.09375
- up_weight: bfloat16 [64, 2048, 4096], P('expert', 'hidden'), may hold values from -0.09375 to 0.09375
- down_weight: bfloat16 [64, 2048, 4096], P('expert', 'hidden'), may hold values from -0.125 to 0.125
- cotangent: bfloat16 [1024, 4096], P('expert', 'hidden'), may hold values from -6 to 6
Outputs:
- mixed: bfloat16 [1024, 4096], P('expert', 'hidden')
- grad_tokens: bfloat16 [1024, 4096], P('expert', 'hidden')
The draws below stay inside these ranges and needn't reach their ends.
Inputs may be any that keep to these rules, and one draw needn't show every extreme that they name: `expert_ids`: each row names 8 different experts. Within the 16 rows of one group no expert is named more than 4 times, and in every draw some expert is named exactly 4 times by some group.
All inputs are finite; a program needn't handle non-finite values.
Results may differ from the reference program's by a relative error of at most 0.024.
Values may be sent and summed in bfloat16 or wider, within the bound.
A program may use at most 32 MiB of HBM per device.

```python
import math
import jax
import jax.numpy as jnp
import numpy as np
from jax import lax

D = 4096
FF = 2048
TOP = 8
TOK_GRP = 16
EXPERTS = 64
CAP = 4
TOKENS = 1024
N_HIDDEN = 16


def levels(key, shape, cuts, least, high):
    factor_of, own = 1.0, jax.random.fold_in(key, 6)
    for position, shards_of in cuts:
        draws = jnp.exp(jax.random.uniform(jax.random.fold_in(own, position), (shards_of,), jnp.float32, least / len(cuts), high / len(cuts)))
        factor_of = factor_of * jnp.repeat(draws, shape[position] // shards_of).reshape([-1 if axis == position else 1 for axis in range(len(shape))])
    return factor_of


def shared_out(rng, own, number, rows, amount, top, reach, skew):
    sequence = jax.random.permutation(rng, amount)
    heavy_load, common = portions_of(amount, rows * top, reach, skew, True), portions_of(amount, rows * top, reach, skew, False)
    places = jnp.arange(amount)

    def named(sizes, turn):
        used = int((sizes > 0).sum())
        fixed = max(1, used // 4)
        shifted = fixed + (places - fixed + turn * (used - fixed)) % max(1, amount - fixed)
        return jnp.zeros((amount,), jnp.int32).at[sequence[jnp.where(places < fixed, places, shifted)]].set(jnp.asarray(sizes, jnp.int32))

    sizes = jnp.where(number % 4 == 0, named(heavy_load, number // 4), named(common, number - number // 4 - 1))
    mixed = jax.random.permutation(jax.random.fold_in(own, 3), amount)
    giver, sink = mixed[0:amount // 2 * 2:2], mixed[1:amount // 2 * 2:2]
    margin = jnp.minimum(sizes[giver] - 1, reach - sizes[sink]) // 2
    margin = jnp.where((giver == sequence[0]) | (sink == sequence[0]) | (sizes[sink] == 0), 0, jnp.maximum(margin, 0))
    shifted = jax.random.randint(jax.random.fold_in(own, 4), (amount // 2,), 0, 1 << 20) % (margin + 1)
    sizes = sizes.at[giver].add(-shifted).at[sink].add(shifted)
    labels = jnp.searchsorted(jnp.cumsum(sizes), jnp.arange(rows * top), side="right").astype(jnp.int32)
    listing = labels.reshape(top, rows).T
    listing = listing[jax.random.permutation(jax.random.fold_in(own, 1), rows)]
    turn = jax.random.randint(jax.random.fold_in(own, 2), (rows, 1), 0, top)
    return jnp.take_along_axis(listing, (jnp.arange(top)[None, :] + turn) % top, axis=1)


def portions_of(number_of, total, most, lean, full):
    weights = [(1 << 20) // math.isqrt(standing ** lean) + 1 for standing in range(1, number_of + 1)]
    largest = most if full else min(most, max(-(-total // number_of), total * weights[0] // sum(weights)))
    least = 1 if total - largest >= number_of - 1 else 0
    counts, spare = [largest] + [least] * (number_of - 1), total - largest - least * (number_of - 1)
    while spare > 0:
        candidates = [i for i in range(1, number_of) if counts[i] < largest] or [i for i in range(1, number_of) if counts[i] < most]
        whole, remaining = sum([weights[i] for i in candidates]), spare
        for i in candidates:
            addition = min(most - counts[i], max(1, remaining * weights[i] // whole), spare)
            counts[i] = counts[i] + addition
            spare = spare - addition
    return np.array(counts)


def gaussian(stream_key, shape, width, most, split=(), held_as=jnp.bfloat16):
    gain = levels(stream_key, shape, split, -0.22, 0.18) if split else 1.0
    entries = jax.random.normal(stream_key, shape, jnp.float32) * width * gain
    return jnp.minimum(jnp.maximum(entries, -most), most).astype(held_as)


def setup_inputs(seed: int = 0) -> dict:
    key_list = jax.random.split(jax.random.key(seed), 8)
    tokens = gaussian(key_list[0], (TOKENS, D), 1.0, 6.0, ((0, 64), (1, 16)))
    probs = jnp.clip(jnp.exp(math.log(0.6) - 2.4849067 * jax.random.uniform(key_list[1], (TOKENS, TOP), jnp.float32) ** levels(key_list[1], (TOKENS, TOP), ((0, 64),), -0.2, 0.2)), 0.05, 0.6)
    expert_ids_keys = jax.random.split(jax.random.fold_in(key_list[2], 1), TOKENS // TOK_GRP)
    expert_ids_turns = jax.random.permutation(jax.random.fold_in(key_list[2], 3), TOKENS // TOK_GRP)
    expert_ids = jax.vmap(lambda own, number: shared_out(jax.random.fold_in(key_list[2], 2), own, number, TOK_GRP, EXPERTS, TOP, CAP, 2))(expert_ids_keys, expert_ids_turns).reshape((TOKENS, TOP))
    gate_weight = gaussian(key_list[3], (EXPERTS, FF, D), D ** -0.5, 0.09375, ((0, 64), (1, 16)))
    up_weight = gaussian(key_list[4], (EXPERTS, FF, D), D ** -0.5, 0.09375, ((0, 64), (1, 16)))
    down_weight = gaussian(key_list[5], (EXPERTS, FF, D), FF ** -0.5, 0.125, ((0, 64), (1, 16)))
    cotangent = gaussian(key_list[6], (TOKENS, D), 1.0, 6.0, ((0, 64), (1, 16)))
    return dict(tokens=tokens, probs=probs, expert_ids=expert_ids, gate_weight=gate_weight, up_weight=up_weight, down_weight=down_weight, cotangent=cotangent)


def reference(tokens, probs, expert_ids, gate_weight, up_weight, down_weight, cotangent):
    groups = TOKENS // TOK_GRP
    pairs = TOK_GRP * TOP
    rows_exp = groups * CAP
    blocks = N_HIDDEN
    block_width = FF // N_HIDDEN
    grouped = expert_ids.reshape(groups, pairs).astype(jnp.int32)
    onehot = (grouped[:, :, None] == jnp.arange(EXPERTS, dtype=jnp.int32)[None, None, :]).astype(jnp.int32)
    earlier = jnp.cumsum(onehot, axis=1) - onehot
    slot_index = jnp.sum(earlier * onehot, axis=2).astype(jnp.int32)
    group_index = jnp.arange(groups, dtype=jnp.int32)[:, None]
    pair_index = jnp.arange(pairs, dtype=jnp.int32)[None, :]
    token_index = (group_index * TOK_GRP + pair_index // TOP).astype(jnp.int32)
    row_position = (group_index * CAP + slot_index).astype(jnp.int32)
    flat_ids = grouped.reshape(-1)
    flat_rows = row_position.reshape(-1)
    table = jnp.full((EXPERTS, rows_exp), -1, jnp.int32).at[flat_ids, flat_rows].set(token_index.reshape(-1))
    weight_table = jnp.zeros((EXPERTS, rows_exp), jnp.float32).at[flat_ids, flat_rows].set(probs.reshape(-1).astype(jnp.float32))
    valid = table >= 0
    safe_index = jnp.maximum(table, 0)

    def one_expert(items):
        expert, index_row, weight_row, valid_row = items
        w_gate = gate_weight[expert]
        w_up = up_weight[expert]
        w_down = down_weight[expert]
        rows_in = jnp.where(valid_row[:, None], tokens[index_row], jnp.zeros((), jnp.bfloat16)).astype(jnp.bfloat16)
        gate = jnp.dot(rows_in, w_gate.T, preferred_element_type=jnp.float32)
        upper = jnp.dot(rows_in, w_up.T, preferred_element_type=jnp.float32)
        hidden = (jax.nn.silu(gate) * upper).astype(jnp.bfloat16)
        hidden_blocks = hidden.reshape(rows_exp, blocks, block_width).astype(jnp.float32)
        down_blocks = w_down.reshape(blocks, block_width, D).astype(jnp.float32)
        pieces = jnp.einsum("rnf,nfd->nrd", hidden_blocks, down_blocks).astype(jnp.bfloat16)
        expert_out = jnp.sum(pieces.astype(jnp.float32), axis=0)
        scaled = (weight_row[:, None] * cotangent[index_row].astype(jnp.float32)).astype(jnp.bfloat16)
        grad_hidden = jnp.dot(scaled, w_down.T, preferred_element_type=jnp.float32)
        sigma = jax.nn.sigmoid(gate)
        grad_gate = (grad_hidden * upper * sigma * (1.0 + gate * (1.0 - sigma))).astype(jnp.bfloat16)
        grad_up = (grad_hidden * gate * sigma).astype(jnp.bfloat16)
        gate_blocks = w_gate.reshape(blocks, block_width, D).astype(jnp.float32)
        up_blocks = w_up.reshape(blocks, block_width, D).astype(jnp.float32)
        grad_pieces = jnp.einsum("rnf,nfd->nrd", grad_gate.reshape(rows_exp, blocks, block_width).astype(jnp.float32), gate_blocks)
        grad_pieces = grad_pieces + jnp.einsum("rnf,nfd->nrd", grad_up.reshape(rows_exp, blocks, block_width).astype(jnp.float32), up_blocks)
        grad_rows = jnp.sum(grad_pieces.astype(jnp.bfloat16).astype(jnp.float32), axis=0)
        return expert_out, grad_rows

    outputs, grads = lax.map(one_expert, (jnp.arange(EXPERTS, dtype=jnp.int32), safe_index, weight_table, valid))
    picked_out = outputs[flat_ids, flat_rows].reshape(TOKENS, TOP, D)
    picked_grad = grads[flat_ids, flat_rows].reshape(TOKENS, TOP, D)
    mixed = jnp.sum(probs.astype(jnp.float32)[:, :, None] * picked_out, axis=1).astype(jnp.bfloat16)
    grad_tokens = jnp.sum(picked_grad, axis=1).astype(jnp.bfloat16)
    return mixed, grad_tokens
```

```python
import functools

import jax
import jax.numpy as jnp
from jax import lax
from jax.experimental import pallas as pl
from jax.experimental.pallas import tpu as pltpu
from jax.sharding import PartitionSpec as P

MESH = pl.DeviceIdType.MESH
CAP = 4
TILE = 16
LANES = 128
CHUNKS = 2
F32 = jnp.float32
BF16 = jnp.bfloat16
DIRS = (1, -1)
NT = (((1,), (1,)), ((), ()))
TN = (((0,), (0,)), ((), ()))


def dot(a, b, dims=(((1,), (0,)), ((), ()))):
    return lax.dot_general(a, b, dims, preferred_element_type=F32)


def iota(shape, axis):
    return lax.broadcasted_iota(jnp.int32, shape, axis)


def routing_matrix(ids, probs, me_e, n_e):
    toks, top = ids.shape
    shape = (toks, n_e * TILE)
    lane = iota(shape, 1)
    expert = lane // TILE + me_e
    expert = jnp.where(expert >= n_e, expert - n_e, expert)
    part = (lane % TILE) // CAP
    slot = (lane % CAP).astype(F32)
    member = jnp.zeros(shape, F32)
    weight = jnp.zeros(shape, F32)
    for k in range(top):
        same = ids[:, k : k + 1] == expert
        member = jnp.where(same, 1.0, member)
        weight = jnp.where(same, probs[:, k : k + 1], weight)
    before = (iota((toks, toks), 1) < iota((toks, toks), 0)).astype(BF16)
    count = dot(before, member.astype(BF16))
    pick = jnp.where(count == slot, member, 0.0)
    weight = pick * weight
    high = weight.astype(BF16).astype(F32)
    middle = (weight - high).astype(BF16).astype(F32)
    low = weight - high - middle
    blocks = []
    for q, value in enumerate((pick, high, middle, low)):
        for half in range(2):
            here = part == (0 if q == 0 else 2) + half
            blocks.append(jnp.where(here, value, 0.0).astype(BF16))
    return jnp.concatenate(blocks, axis=0)


def permutation(size, inverse):
    seg = size // 4
    o = iota((size, size), 1 if inverse else 0)
    i = iota((size, size), 0 if inverse else 1)
    rest = o % seg
    return (i == (rest // CAP) * TILE + (o // seg) * CAP + rest % CAP).astype(BF16)


def kernel(
    n_e, n_h, tok_ref, probs_ref, ids_ref, gate_hbm, up_hbm, down_hbm, cot_ref,
    mixed_ref, grad_ref,
    w_gu, w_down, route, send, recv, back, ret, rows, sib_out, sib_in, rs_out, rs_in, act,
    w_sem, a2a_sem, ret_sem, ag_send, ag_recv, fw_send, fw_recv, sx_send, sx_recv, rs_send, rs_recv,
):
    n_x = n_h // 2
    steps = n_x // 2
    toks, width = tok_ref.shape
    hid = gate_hbm.shape[1]
    n_rows = n_e * CAP
    piece = n_rows // CHUNKS
    group = min(16, n_e)
    me_e = lax.axis_index("expert")
    me_h = lax.axis_index("hidden")
    x = me_h // 2
    core = me_h % 2

    def at(rel, other=False):
        return ((x + (rel + n_x)) % n_x) * 2 + (1 - core if other else core)

    sibling = (me_e, x * 2 + 1 - core)

    barrier = pltpu.get_barrier_semaphore()

    def greet(j, carry):
        pl.semaphore_signal(barrier, inc=1, device_id=((me_e + j) % n_e, me_h), device_id_type=MESH)
        return carry

    lax.fori_loop(1, n_e, greet, 0)
    for d in DIRS:
        pl.semaphore_signal(barrier, inc=1, device_id=(me_e, at(d)), device_id_type=MESH)
    pl.semaphore_signal(barrier, inc=1, device_id=sibling, device_id_type=MESH)

    loads = [
        pltpu.make_async_copy(gate_hbm.at[0], w_gu.at[pl.ds(0, hid)], w_sem.at[0]),
        pltpu.make_async_copy(up_hbm.at[0], w_gu.at[pl.ds(hid, hid)], w_sem.at[1]),
        pltpu.make_async_copy(down_hbm.at[0], w_down, w_sem.at[2]),
    ]
    for load in loads:
        load.start()

    route[...] = routing_matrix(ids_ref[...], probs_ref[...], me_e, n_e)
    halves = lambda v: [v[:, :LANES], v[:, LANES:]]
    source = jnp.concatenate(halves(tok_ref[...]) + halves(cot_ref[...]) * 3, axis=0)
    send[...] = dot(route[...], source, TN).astype(BF16)

    pl.semaphore_wait(barrier, n_e + 2)

    def message(j, src, dst, sems, sign):
        place = pl.ds(pl.multiple_of(j * TILE, TILE), TILE)
        return pltpu.make_async_remote_copy(
            src_ref=src.at[place], dst_ref=dst.at[place], send_sem=sems.at[0], recv_sem=sems.at[1],
            device_id=((me_e + sign * j + n_e) % n_e, me_h), device_id_type=MESH,
        )

    def all_messages(src, dst, sems):
        place = pl.ds(TILE, (n_e - 1) * TILE)
        return pltpu.make_async_remote_copy(
            src_ref=src.at[place], dst_ref=dst.at[place], send_sem=sems.at[0], recv_sem=sems.at[1],
            device_id=((me_e + 1) % n_e, me_h), device_id_type=MESH,
        )

    def dispatch(j, carry):
        message(j, send, recv, a2a_sem, 1).start()
        return carry

    lax.fori_loop(1, n_e, dispatch, 0)
    recv[pl.ds(0, TILE)] = send[pl.ds(0, TILE)]
    order = permutation(group * TILE, False)
    all_messages(send, recv, a2a_sem).wait_recv()
    seg = group * CAP
    for g in range(n_e // group):
        sorted_rows = dot(order, recv[pl.ds(g * group * TILE, group * TILE)]).astype(BF16)
        for a in range(2):
            for half in range(2):
                q = a * 2 + half
                rows[a, me_h, pl.ds(g * seg, seg), pl.ds(half * LANES, LANES)] = sorted_rows[q * seg : (q + 1) * seg]

    def part(p):
        return pl.ds(p * piece, piece)

    def parts_of(d, k):
        if k < steps:
            return range(CHUNKS)
        return range(CHUNKS // 2) if d == 1 else range(CHUNKS // 2, CHUNKS)

    def ag(a, d, k, p, arriving=False):
        where = rows.at[a, at(-k * d if arriving else -(k - 1) * d), part(p)]
        i = 0 if d == 1 else 1
        return pltpu.make_async_remote_copy(
            src_ref=where, dst_ref=where, send_sem=ag_send.at[a, i, k - 1, p], recv_sem=ag_recv.at[a, i, k - 1, p],
            device_id=(me_e, at(d)), device_id_type=MESH,
        )

    def fw(a, rel, p, arriving=False):
        where = rows.at[a, at(rel, arriving), part(p)]
        return pltpu.make_async_remote_copy(
            src_ref=where, dst_ref=where, send_sem=fw_send.at[a, rel % n_x, p], recv_sem=fw_recv.at[a, rel % n_x, p],
            device_id=sibling, device_id_type=MESH,
        )

    def ag_begin(a):
        for p in range(CHUNKS):
            for d in DIRS:
                ag(a, d, 1, p).start()
        for p in range(CHUNKS):
            fw(a, 0, p).start()

    def ag_step(a, k):
        for p in range(CHUNKS):
            for d in DIRS:
                if p in parts_of(d, k):
                    ag(a, d, k, p, True).wait_recv()
                    if k < steps and p in parts_of(d, k + 1):
                        ag(a, d, k + 1, p).start()
                    fw(a, -k * d, p).start()

    def rels(k):
        return (0,) if k == 0 else (k,) if k == steps else (-k, k)

    def cols(h):
        return pl.ds(pl.multiple_of(h * width, width), width)

    def ag_multiply(a, k, total, weights):
        for rel in rels(k):
            for other in (False, True):
                if other:
                    for p in range(CHUNKS):
                        fw(a, rel, p, True).wait_recv()
                h = at(rel, other)
                term = dot(rows[a, h], weights[:, cols(h)], NT)
                total = term if total is None else total + term
        return total

    def own(b, rel, other):
        left = act[b, :, :hid] if b == 0 else act[b]
        right = w_down if b == 0 else w_gu
        return dot(left, right[:, cols(at(rel, other))])

    def sx(b, rel):
        i = rel % n_x
        return pltpu.make_async_remote_copy(
            src_ref=sib_out.at[b, i], dst_ref=sib_in.at[b, i], send_sem=sx_send.at[b, i], recv_sem=sx_recv.at[b, i],
            device_id=sibling, device_id_type=MESH,
        )

    far_first = [steps] + [s * k for k in range(steps - 1, 0, -1) for s in (1, -1)] + [0]

    def rs_exchange(b):
        for rel in far_first:
            sib_out[b, rel % n_x] = own(b, rel, True).astype(BF16)
            sx(b, rel).start()

    def rs(b, d, j, p):
        i = 0 if d == 1 else 1
        return pltpu.make_async_remote_copy(
            src_ref=rs_out.at[b, i, j, part(p)], dst_ref=rs_in.at[b, i, j, part(p)],
            send_sem=rs_send.at[b, i, j, p], recv_sem=rs_recv.at[b, i, j, p],
            device_id=(me_e, at(d)), device_id_type=MESH,
        )

    def rs_step(b, j):
        if j == 0:
            sx(b, steps).wait_recv()
            mine = own(b, steps, False)
            both = [mine, mine]
        else:
            both = []
            for d in DIRS:
                sx(b, (steps - j) * d).wait_recv()
                both.append(own(b, (steps - j) * d, False))
        for p in range(CHUNKS):
            for i, d in enumerate(DIRS):
                rel = steps if j == 0 else (steps - j) * d
                if p not in parts_of(d, steps - j):
                    continue
                value = both[i][p * piece : (p + 1) * piece] + sib_in[b, rel % n_x, part(p)].astype(F32)
                if j > 0 and p in parts_of(d, steps - j + 1):
                    rs(b, d, j - 1, p).wait_recv()
                    value = value + rs_in[b, i, j - 1, part(p)].astype(F32)
                rs_out[b, i, j, part(p)] = value.astype(BF16)
                rs(b, d, j, p).start()

    def rs_last(b):
        sx(b, 0).wait_recv()
        total = own(b, 0, False) + sib_in[b, 0].astype(F32)
        for i, d in enumerate(DIRS):
            for p in parts_of(d, 1):
                rs(b, d, steps - 1, p).wait_recv()
        got = [rs_in[b, i, steps - 1].astype(F32) for i in range(2)]
        return total + got[0] + got[1]

    ag_begin(0)
    for load in loads:
        load.wait()
    gate_up = ag_multiply(0, 0, None, w_gu)
    for k in range(1, steps + 1):
        ag_step(0, k)
        if k == steps - 1:
            ag_begin(1)
        gate_up = ag_multiply(0, k, gate_up, w_gu)
    gate, up = gate_up[:, :hid], gate_up[:, hid:]
    sigma = 1.0 / (1.0 + jnp.exp(-gate))
    silu = gate * sigma
    act[0, :, :hid] = (silu * up).astype(BF16)
    rs_exchange(0)
    grad_hidden = ag_multiply(1, 0, None, w_down)
    for k in range(1, steps + 1):
        ag_step(1, k)
        if k == steps:
            rs_step(0, 0)
        grad_hidden = ag_multiply(1, k, grad_hidden, w_down)
    act[1, :, :hid] = (grad_hidden * up * sigma * (1.0 + gate * (1.0 - sigma))).astype(BF16)
    act[1, :, hid:] = (grad_hidden * silu).astype(BF16)
    for j in range(1, steps):
        if j == 1:
            rs_exchange(1)
        rs_step(0, j)
    rs_step(1, 0)
    out = rs_last(0).astype(BF16)
    for j in range(1, steps):
        rs_step(1, j)
    grad = rs_last(1).astype(BF16)

    order = permutation(group * TILE, True)
    for g in range(n_e // group):
        stack = jnp.concatenate(
            [v[g * seg : (g + 1) * seg, half * LANES : (half + 1) * LANES] for v in (grad, out) for half in range(2)],
            axis=0,
        )
        back[pl.ds(g * group * TILE, group * TILE)] = dot(order, stack).astype(BF16)

    def give_back(j, carry):
        message(j, back, ret, ret_sem, -1).start()
        return carry

    lax.fori_loop(1, n_e, give_back, 0)
    ret[pl.ds(0, TILE)] = back[pl.ds(0, TILE)]
    all_messages(back, ret, ret_sem).wait_recv()
    result = dot(route[...], ret[...])
    block = lambda q, half: result[(q * 2 + half) * toks : (q * 2 + half + 1) * toks]
    for half in range(2):
        where = pl.ds(half * LANES, LANES)
        grad_ref[:, where] = block(0, half).astype(grad_ref.dtype)
        mixed_ref[:, where] = (block(1, half) + block(2, half) + block(3, half)).astype(mixed_ref.dtype)

    all_messages(send, recv, a2a_sem).wait_send()
    all_messages(back, ret, ret_sem).wait_send()
    for b in range(2):
        for d in DIRS:
            for k in range(1, steps + 1):
                for p in parts_of(d, k):
                    ag(b, d, k, p).wait_send()
                    rs(b, d, steps - k, p).wait_send()
        for rel in range(n_x):
            sx(b, rel).wait_send()
            for p in range(CHUNKS):
                fw(b, rel, p).wait_send()


def shards(tokens, probs, expert_ids, gate_weight, up_weight, down_weight, cotangent):
    n_e, n_h = lax.axis_size("expert"), lax.axis_size("hidden")
    n_x = n_h // 2
    steps = n_x // 2
    width = tokens.shape[1]
    hid, feats = gate_weight.shape[1:]
    n_rows = n_e * CAP
    dma = pltpu.SemaphoreType.DMA
    vmem = pl.BlockSpec(memory_space=pltpu.VMEM)
    hbm = pl.BlockSpec(memory_space=pl.ANY)
    messages = pltpu.VMEM((n_e * TILE, LANES), BF16)
    return pl.pallas_call(
        functools.partial(kernel, n_e, n_h),
        out_shape=(
            jax.ShapeDtypeStruct(tokens.shape, tokens.dtype),
            jax.ShapeDtypeStruct(tokens.shape, tokens.dtype),
        ),
        in_specs=[vmem, vmem, vmem, hbm, hbm, hbm, vmem],
        out_specs=(vmem, vmem),
        scratch_shapes=[
            pltpu.VMEM((2 * hid, feats), BF16),
            pltpu.VMEM((hid, feats), BF16),
            pltpu.VMEM((8 * tokens.shape[0], n_e * TILE), BF16),
            messages,
            messages,
            messages,
            messages,
            pltpu.VMEM((2, n_h, n_rows, width), BF16),
            pltpu.VMEM((2, n_x, n_rows, width), BF16),
            pltpu.VMEM((2, n_x, n_rows, width), BF16),
            pltpu.VMEM((2, 2, steps, n_rows, width), BF16),
            pltpu.VMEM((2, 2, steps, n_rows, width), BF16),
            pltpu.VMEM((2, n_rows, 2 * hid), BF16),
            dma((3,)),
            dma((2,)),
            dma((2,)),
            dma((2, 2, steps, CHUNKS)),
            dma((2, 2, steps, CHUNKS)),
            dma((2, n_x, CHUNKS)),
            dma((2, n_x, CHUNKS)),
            dma((2, n_x)),
            dma((2, n_x)),
            dma((2, 2, steps, CHUNKS)),
            dma((2, 2, steps, CHUNKS)),
        ],
        compiler_params=pltpu.CompilerParams(
            collective_id=0, has_side_effects=True, vmem_limit_bytes=48 * 1024 * 1024
        ),
    )(tokens, probs, expert_ids, gate_weight, up_weight, down_weight, cotangent)


def solution(mesh):
    placed = (
        P("expert", "hidden"),
        P("expert", None),
        P("expert", None),
        P("expert", "hidden", None),
        P("expert", "hidden", None),
        P("expert", "hidden", None),
        P("expert", "hidden"),
    )
    return jax.shard_map(
        shards,
        mesh=mesh,
        in_specs=placed,
        out_specs=(P("expert", "hidden"), P("expert", "hidden")),
        check_vma=False,
    )
```

```python
import functools

import jax
import jax.numpy as jnp
from jax import lax
from jax.experimental import pallas as pl
from jax.experimental.pallas import tpu as pltpu
from jax.sharding import PartitionSpec as P

MESH = pl.DeviceIdType.MESH
CAP = 4
TILE = 16
LANES = 128
CHUNKS = 2
F32 = jnp.float32
BF16 = jnp.bfloat16
DIRS = (1, -1)
NT = (((1,), (1,)), ((), ()))
TN = (((0,), (0,)), ((), ()))


def dot(a, b, dims=(((1,), (0,)), ((), ()))):
    return lax.dot_general(a, b, dims, preferred_element_type=F32)


def iota(shape, axis):
    return lax.broadcasted_iota(jnp.int32, shape, axis)


def routing_matrix(ids_t, probs_t, me_e, n_e):
    top, toks = ids_t.shape
    unit = (iota((top, top), 0) == iota((top, top), 1)).astype(BF16)
    turn = lambda v: dot(v.astype(BF16), unit, TN)
    ids = turn(ids_t.astype(F32)).astype(jnp.int32)
    high = probs_t.astype(BF16).astype(F32)
    middle = (probs_t - high).astype(BF16).astype(F32)
    probs = [turn(v) for v in (high, middle, probs_t - high - middle)]
    shape = (toks, n_e * TILE)
    lane = iota(shape, 1)
    expert = lane // TILE + me_e
    expert = jnp.where(expert >= n_e, expert - n_e, expert)
    part = (lane % TILE) // CAP
    slot = (lane % CAP).astype(F32)
    member = jnp.zeros(shape, F32)
    weights = [jnp.zeros(shape, F32)] * 3
    for k in range(top):
        same = ids[:, k : k + 1] == expert
        member = jnp.where(same, 1.0, member)
        weights = [jnp.where(same, v[:, k : k + 1], w) for v, w in zip(probs, weights)]
    before = (iota((toks, toks), 1) < iota((toks, toks), 0)).astype(BF16)
    count = dot(before, member.astype(BF16))
    pick = jnp.where(count == slot, member, 0.0)
    blocks = []
    for q, value in enumerate([pick] + [pick * w for w in weights]):
        for half in range(2):
            here = part == (0 if q == 0 else 2) + half
            blocks.append(jnp.where(here, value, 0.0).astype(BF16))
    return jnp.concatenate(blocks, axis=0)


def permutation(size, inverse):
    seg = size // 4
    o = iota((size, size), 1 if inverse else 0)
    i = iota((size, size), 0 if inverse else 1)
    rest = o % seg
    return (i == (rest // CAP) * TILE + (o // seg) * CAP + rest % CAP).astype(BF16)


def kernel(
    n_e, n_h, tok_hbm, probs_hbm, ids_hbm, gate_hbm, up_hbm, down_hbm, cot_hbm,
    mixed_ref, grad_ref,
    tok_ref, cot_ref, probs_ref, ids_ref,
    w_gu, w_down, route, send, recv, back, ret, send_far, recv_far, back_far, ret_far, raw, far_out, far_in, rows, sib_out, sib_in, rs_out, rs_in, act, fin, fin_far,
    w_sem, small_sem, a2a_send, a2a_recv, ret_send, ret_recv, a2a_far_send, a2a_far_recv, ret_far_send, ret_far_recv,
    cross_send, cross_recv,
    ag_send, ag_recv, fw_send, fw_recv, sx_send, sx_recv, rs_send, rs_recv,
):
    n_x = n_h // 2
    far = n_x // 2
    steps = far - 1
    toks, width = tok_ref.shape
    hid = gate_hbm.shape[1]
    piece = n_e * CAP // CHUNKS
    groups = n_e // CHUNKS
    block = min(16, groups)
    me_e = lax.axis_index("expert")
    me_h = lax.axis_index("hidden")
    x = me_h // 2
    core = me_h % 2

    def at(rel, other=False):
        return ((x + (rel + n_x)) % n_x) * 2 + (1 - core if other else core)

    sibling = (me_e, x * 2 + 1 - core)

    barrier = pltpu.get_barrier_semaphore()

    def greet(j, carry):
        pl.semaphore_signal(barrier, inc=1, device_id=((me_e + j) % n_e, me_h), device_id_type=MESH)
        return carry

    for d in DIRS:
        pl.semaphore_signal(barrier, inc=1, device_id=(me_e, at(d)), device_id_type=MESH)
    pl.semaphore_signal(barrier, inc=1, device_id=(me_e, at(far)), device_id_type=MESH)
    pl.semaphore_signal(barrier, inc=1, device_id=sibling, device_id_type=MESH)
    lax.fori_loop(1, n_e, greet, 0)

    small = [
        pltpu.make_async_copy(src, dst, small_sem.at[i])
        for i, (src, dst) in enumerate(
            ((ids_hbm, ids_ref), (probs_hbm, probs_ref), (tok_hbm, tok_ref), (cot_hbm, cot_ref))
        )
    ]
    loads = [
        pltpu.make_async_copy(gate_hbm.at[0], w_gu.at[pl.ds(0, hid)], w_sem.at[0]),
        pltpu.make_async_copy(up_hbm.at[0], w_gu.at[pl.ds(hid, hid)], w_sem.at[1]),
        pltpu.make_async_copy(down_hbm.at[0], w_down, w_sem.at[2]),
    ]
    for load in small + loads:
        load.start()
    for load in small:
        load.wait()

    route[...] = routing_matrix(ids_ref[...], probs_ref[...], me_e, n_e)
    halves = lambda v: [v[:, :LANES], v[:, LANES:]]

    def placed(tok, cot):
        source = jnp.concatenate(halves(tok) + halves(cot) * 3, axis=0)
        return dot(route[...], source, TN).astype(BF16)

    send[...] = placed(tok_ref[...], cot_ref[...])
    for load in loads:
        load.wait()

    pl.semaphore_wait(barrier, n_e + 3)

    def message(j, p, src, dst, sems, sign):
        place = pl.ds(pl.multiple_of(j * TILE, TILE), TILE)
        return pltpu.make_async_remote_copy(
            src_ref=src.at[place], dst_ref=dst.at[place], send_sem=sems[0].at[p], recv_sem=sems[1].at[p],
            device_id=((me_e + sign * j + n_e) % n_e, me_h), device_id_type=MESH,
        )

    def first(p):
        return 1 if p == 0 else p * groups

    def post(p, src, dst, sems, sign):
        def one(j, carry):
            message(j, p, src, dst, sems, sign).start()
            return carry

        lax.fori_loop(first(p), (p + 1) * groups, one, 0)

    def posted(p, src, dst, sems):
        place = pl.ds(first(p) * TILE, ((p + 1) * groups - first(p)) * TILE)
        return pltpu.make_async_remote_copy(
            src_ref=src.at[place], dst_ref=dst.at[place], send_sem=sems[0].at[p], recv_sem=sems[1].at[p],
            device_id=((me_e + 1) % n_e, me_h), device_id_type=MESH,
        )

    out_way = (send, recv, (a2a_send, a2a_recv))
    home_way = (back, ret, (ret_send, ret_recv))
    out_far = (send_far, recv_far, (a2a_far_send, a2a_far_recv))
    home_far = (back_far, ret_far, (ret_far_send, ret_far_recv))

    def cross(i, src, dst):
        return pltpu.make_async_remote_copy(
            src_ref=src, dst_ref=dst, send_sem=cross_send.at[i], recv_sem=cross_recv.at[i],
            device_id=(me_e, at(far)), device_id_type=MESH,
        )

    crossing = [cross(0, tok_ref, raw.at[0]), cross(1, cot_ref, raw.at[1]), cross(2, far_out, far_in)]

    def part(p):
        return pl.ds(p * piece, piece)

    seg = block * CAP
    order = permutation(block * TILE, False)

    def arrive(p, way, rel):
        posted(p, *way).wait_recv()
        for g in range(p * groups // block, (p + 1) * groups // block):
            sorted_rows = dot(order, way[1][pl.ds(g * block * TILE, block * TILE)]).astype(BF16)
            for a in range(2):
                for half in range(2):
                    q = a * 2 + half
                    rows[a, at(rel), pl.ds(g * seg, seg), pl.ds(half * LANES, LANES)] = sorted_rows[q * seg : (q + 1) * seg]

    def ag(a, p, d, k, arriving=False):
        where = rows.at[a, at(-k * d if arriving else -(k - 1) * d), part(p)]
        i = 0 if d == 1 else 1
        return pltpu.make_async_remote_copy(
            src_ref=where, dst_ref=where, send_sem=ag_send.at[a, i, k - 1, p], recv_sem=ag_recv.at[a, i, k - 1, p],
            device_id=(me_e, at(d)), device_id_type=MESH,
        )

    def fw(a, p, rel, arriving=False):
        where = rows.at[a, at(rel, arriving), part(p)]
        return pltpu.make_async_remote_copy(
            src_ref=where, dst_ref=where, send_sem=fw_send.at[a, rel % n_x, p], recv_sem=fw_recv.at[a, rel % n_x, p],
            device_id=sibling, device_id_type=MESH,
        )

    def gather(a, p, k):
        for d in DIRS:
            if k:
                ag(a, p, d, k, True).wait_recv()
            if k < steps:
                ag(a, p, d, k + 1).start()
            if k:
                fw(a, p, -k * d).start()
        if not k:
            fw(a, p, 0).start()

    def gather_far(p):
        arrive(p, out_far, far)
        for a in range(2):
            fw(a, p, far).start()

    def cols(h):
        return pl.ds(pl.multiple_of(h * width, width), width)

    sums = {}

    def multiply(a, p, k):
        weights = w_down if a else w_gu
        for rel in (-k, k) if 0 < k < far else (k,):
            for other in (False, True):
                if other:
                    fw(a, p, rel, True).wait_recv()
                h = at(rel, other)
                term = dot(rows[a, h, part(p)], weights[:, cols(h)], NT)
                sums[a, p] = sums[a, p] + term if (a, p) in sums else term

    def own(b, p, rel, other):
        left = act[b, part(p)] if b else act[b, part(p), :hid]
        right = w_gu if b else w_down
        return dot(left, right[:, cols(at(rel, other))])

    def sx(b, p, rel):
        i = rel % n_x
        return pltpu.make_async_remote_copy(
            src_ref=sib_out.at[b, i, part(p)], dst_ref=sib_in.at[b, i, part(p)],
            send_sem=sx_send.at[b, i, p], recv_sem=sx_recv.at[b, i, p],
            device_id=sibling, device_id_type=MESH,
        )

    def exchange(b, p, k):
        for rel in (k, -k) if 0 < k < far else (k,):
            sib_out[b, rel % n_x, part(p)] = own(b, p, rel, True).astype(BF16)
            sx(b, p, rel).start()

    def forward_act(p):
        gate, up = sums[0, p][:, :hid], sums[0, p][:, hid:]
        sigma = 1.0 / (1.0 + jnp.exp(-gate))
        act[0, part(p), :hid] = (gate * sigma * up).astype(BF16)
        exchange(0, p, steps)

    def backward_act(p):
        gate, up = sums[0, p][:, :hid], sums[0, p][:, hid:]
        sigma = 1.0 / (1.0 + jnp.exp(-gate))
        act[1, part(p), :hid] = (sums[1, p] * up * sigma * (1.0 + gate * (1.0 - sigma))).astype(BF16)
        act[1, part(p), hid:] = (sums[1, p] * gate * sigma).astype(BF16)
        exchange(1, p, steps)

    def rs(b, p, d, j):
        i = 0 if d == 1 else 1
        return pltpu.make_async_remote_copy(
            src_ref=rs_out.at[b, i, j, part(p)], dst_ref=rs_in.at[b, i, j, part(p)],
            send_sem=rs_send.at[b, i, j, p], recv_sem=rs_recv.at[b, i, j, p],
            device_id=(me_e, at(d)), device_id_type=MESH,
        )

    def pair_sum(b, p, rel):
        value = own(b, p, rel, False)
        sx(b, p, rel).wait_recv()
        return value + sib_in[b, rel % n_x, part(p)].astype(F32)

    def reduce(b, p, j):
        for i, d in enumerate(DIRS):
            value = pair_sum(b, p, (steps - j) * d)
            if j > 0:
                rs(b, p, d, j - 1).wait_recv()
                value = value + rs_in[b, i, j - 1, part(p)].astype(F32)
            rs_out[b, i, j, part(p)] = value.astype(BF16)
            rs(b, p, d, j).start()

    def finish(b, p):
        value = pair_sum(b, p, 0)
        for i, d in enumerate(DIRS):
            rs(b, p, d, steps - 1).wait_recv()
            value = value + rs_in[b, i, steps - 1, part(p)].astype(F32)
        fin[b, part(p)] = value.astype(BF16)

    def finish_far(p):
        for b in range(2):
            fin_far[b, part(p)] = pair_sum(b, p, far).astype(BF16)
        give_back(p, fin_far, home_far)

    inverse = permutation(block * TILE, True)

    def give_back(p, whole, way):
        for g in range(p * groups // block, (p + 1) * groups // block):
            stack = jnp.concatenate(
                [whole[b, pl.ds(g * seg, seg), pl.ds(half * LANES, LANES)] for b in (1, 0) for half in range(2)], axis=0
            )
            way[0][pl.ds(g * block * TILE, block * TILE)] = dot(inverse, stack).astype(BF16)
        post(p, *way, -1)
        if p == 0:
            way[1][pl.ds(0, TILE)] = way[0][pl.ds(0, TILE)]

    crossing[0].start()
    crossing[1].start()
    for p in range(CHUNKS):
        post(p, *out_way, 1)
    recv[pl.ds(0, TILE)] = send[pl.ds(0, TILE)]
    crossing[0].wait_recv()
    crossing[1].wait_recv()
    send_far[...] = placed(raw[0], raw[1])
    recv_far[pl.ds(0, TILE)] = send_far[pl.ds(0, TILE)]
    late = []
    for p in range(CHUNKS):
        arrive(p, out_way, 0)
        for a in range(2):
            gather(a, p, 0)
            late.append((a, p, 0))
        post(p, *out_far, 1)
    units = list(late)
    for k in range(1, steps + 1):
        for a, p, _ in units:
            gather(a, p, k)
            if k == max(1, steps - 1) and a == 1:
                gather_far(p)
                late += [(0, p, far), (1, p, far)]
            for unit in late[:2]:
                multiply(*unit)
            late = late[2:] + [(a, p, k)]
    todo = []
    for a, p, _ in units:
        for unit in [u for u in late if u[:2] == (a, p)]:
            multiply(*unit)
        (backward_act if a else forward_act)(p)
        for unit in todo:
            reduce(*unit)
        todo = [(a, p, 0)]
    for unit in todo:
        reduce(*unit)
    for j in range(1, steps):
        for b, p, _ in units:
            exchange(b, p, steps - j)
            reduce(b, p, j)
        for b, p, _ in units:
            if j == 1:
                exchange(b, p, far)
    if steps < 2:
        for b, p, _ in units:
            exchange(b, p, far)
    for p in range(CHUNKS):
        finish_far(p)
    for b, p, _ in units:
        exchange(b, p, 0)
    for b, p, _ in units:
        finish(b, p)
        if b:
            give_back(p, fin, home_way)

    def combine(way):
        total = None
        for p in range(CHUNKS):
            posted(p, *way).wait_recv()
            place = pl.ds(p * groups * TILE, groups * TILE)
            term = dot(route[:, place], way[1][place])
            total = term if total is None else total + term
        rows_of = lambda q, half: total[(q * 2 + half) * toks : (q * 2 + half + 1) * toks]
        grad = [rows_of(0, half) for half in range(2)]
        return grad, [rows_of(1, half) + rows_of(2, half) + rows_of(3, half) for half in range(2)]

    for i, pair in enumerate(combine(home_far)):
        for half in range(2):
            far_out[pl.ds(i * toks, toks), pl.ds(half * LANES, LANES)] = pair[half]
    crossing[2].start()
    near = combine(home_way)
    crossing[2].wait_recv()
    for i, (pair, out) in enumerate(zip(near, (grad_ref, mixed_ref))):
        for half in range(2):
            where = pl.ds(half * LANES, LANES)
            out[:, where] = (pair[half] + far_in[pl.ds(i * toks, toks), where]).astype(out.dtype)

    for copy in crossing:
        copy.wait_send()
    for p in range(CHUNKS):
        for way in (out_way, home_way, out_far, home_far):
            posted(p, *way).wait_send()
        for b in range(2):
            for k in range(1, steps + 1):
                for d in DIRS:
                    ag(b, p, d, k).wait_send()
                    rs(b, p, d, steps - k).wait_send()
            for rel in range(n_x):
                sx(b, p, rel).wait_send()
                fw(b, p, rel).wait_send()


def shards(tokens, probs, expert_ids, gate_weight, up_weight, down_weight, cotangent):
    n_e, n_h = lax.axis_size("expert"), lax.axis_size("hidden")
    n_x = n_h // 2
    steps = n_x // 2 - 1
    width = tokens.shape[1]
    hid, feats = gate_weight.shape[1:]
    n_rows = n_e * CAP
    dma = pltpu.SemaphoreType.DMA
    vmem = pl.BlockSpec(memory_space=pltpu.VMEM)
    hbm = pl.BlockSpec(memory_space=pltpu.HBM)
    messages = pltpu.VMEM((n_e * TILE, LANES), BF16)
    return pl.pallas_call(
        functools.partial(kernel, n_e, n_h),
        out_shape=(
            jax.ShapeDtypeStruct(tokens.shape, tokens.dtype),
            jax.ShapeDtypeStruct(tokens.shape, tokens.dtype),
        ),
        in_specs=[hbm] * 7,
        out_specs=(vmem, vmem),
        scratch_shapes=[
            pltpu.VMEM(tokens.shape, BF16),
            pltpu.VMEM(tokens.shape, BF16),
            pltpu.VMEM(probs.shape[::-1], F32),
            pltpu.VMEM(probs.shape[::-1], jnp.int32),
            pltpu.VMEM((2 * hid, feats), BF16),
            pltpu.VMEM((hid, feats), BF16),
            pltpu.VMEM((8 * tokens.shape[0], n_e * TILE), BF16),
            *[messages] * 8,
            pltpu.VMEM((2, *tokens.shape), BF16),
            pltpu.VMEM((2 * tokens.shape[0], width), F32),
            pltpu.VMEM((2 * tokens.shape[0], width), F32),
            pltpu.VMEM((2, n_h, n_rows, width), BF16),
            pltpu.VMEM((2, n_x, n_rows, width), BF16),
            pltpu.VMEM((2, n_x, n_rows, width), BF16),
            pltpu.VMEM((2, 2, steps, n_rows, width), BF16),
            pltpu.VMEM((2, 2, steps, n_rows, width), BF16),
            pltpu.VMEM((2, n_rows, 2 * hid), BF16),
            pltpu.VMEM((2, n_rows, width), BF16),
            pltpu.VMEM((2, n_rows, width), BF16),
            dma((3,)),
            dma((4,)),
            *[dma((CHUNKS,))] * 8,
            dma((3,)),
            dma((3,)),
            dma((2, 2, steps, CHUNKS)),
            dma((2, 2, steps, CHUNKS)),
            dma((2, n_x, CHUNKS)),
            dma((2, n_x, CHUNKS)),
            dma((2, n_x, CHUNKS)),
            dma((2, n_x, CHUNKS)),
            dma((2, 2, steps, CHUNKS)),
            dma((2, 2, steps, CHUNKS)),
        ],
        compiler_params=pltpu.CompilerParams(
            collective_id=0, has_side_effects=True, vmem_limit_bytes=63 * 1024 * 1024
        ),
    )(tokens, probs.T, expert_ids.T, gate_weight, up_weight, down_weight, cotangent)


def solution(mesh):
    placed = (
        P("expert", "hidden"),
        P("expert", None),
        P("expert", None),
        P("expert", "hidden", None),
        P("expert", "hidden", None),
        P("expert", "hidden", None),
        P("expert", "hidden"),
    )
    return jax.shard_map(
        shards,
        mesh=mesh,
        in_specs=placed,
        out_specs=(P("expert", "hidden"), P("expert", "hidden")),
        check_vma=False,
    )
```

```python
import functools
import math

import jax
import jax.numpy as jnp
from jax import lax
from jax.experimental import pallas as pl
from jax.experimental.pallas import tpu as pltpu
from jax.sharding import PartitionSpec as P

MESH = pl.DeviceIdType.MESH
CAP = 4
TILE = 16
LANES = 128
CHUNKS = 2
F32 = jnp.float32
BF16 = jnp.bfloat16
DIRS = (1, -1)
NT = (((1,), (1,)), ((), ()))
TN = (((0,), (0,)), ((), ()))


def dot(a, b, dims=(((1,), (0,)), ((), ()))):
    return lax.dot_general(a, b, dims, preferred_element_type=F32)


def iota(shape, axis):
    return lax.broadcasted_iota(jnp.int32, shape, axis)


def torus(n_e):
    rows = math.isqrt(n_e)
    return rows, n_e // rows, (0, 1, 7, 4, 2, 6, 3, 5) if rows == 8 else tuple(range(rows))


def routing_matrix(ids_t, probs_t, me_e, n_e):
    top, toks = ids_t.shape
    unit = (iota((top, top), 0) == iota((top, top), 1)).astype(BF16)
    turn = lambda v: dot(v.astype(BF16), unit, TN)
    ids = turn(ids_t.astype(F32)).astype(jnp.int32)
    high = probs_t.astype(BF16).astype(F32)
    middle = (probs_t - high).astype(BF16).astype(F32)
    probs = [turn(v) for v in (high, middle, probs_t - high - middle)]
    shape = (toks, n_e * TILE)
    lane = iota(shape, 1)
    n_y, n_z, order = torus(n_e)
    place = lane // TILE
    y = jnp.zeros(shape, jnp.int32)
    for i, dy in enumerate(order):
        y = jnp.where(place // n_z == i, (me_e // n_z + dy) % n_y, y)
    expert = y * n_z + (place % n_z + me_e) % n_z
    part = (lane % TILE) // CAP
    slot = (lane % CAP).astype(F32)
    member = jnp.zeros(shape, F32)
    weights = [jnp.zeros(shape, F32)] * 3
    for k in range(top):
        same = ids[:, k : k + 1] == expert
        member = jnp.where(same, 1.0, member)
        weights = [jnp.where(same, v[:, k : k + 1], w) for v, w in zip(probs, weights)]
    before = (iota((toks, toks), 1) < iota((toks, toks), 0)).astype(BF16)
    count = dot(before, member.astype(BF16))
    pick = jnp.where(count == slot, member, 0.0)
    blocks = []
    for q, value in enumerate([pick] + [pick * w for w in weights]):
        for half in range(2):
            here = part == (0 if q == 0 else 2) + half
            blocks.append(jnp.where(here, value, 0.0).astype(BF16))
    return jnp.concatenate(blocks, axis=0)


def permutation(size, inverse):
    seg = size // 4
    o = iota((size, size), 1 if inverse else 0)
    i = iota((size, size), 0 if inverse else 1)
    rest = o % seg
    return (i == (rest // CAP) * TILE + (o // seg) * CAP + rest % CAP).astype(BF16)


def kernel(
    n_e, n_h, tok_hbm, probs_hbm, ids_hbm, gate_hbm, up_hbm, down_hbm, cot_hbm,
    mixed_ref, grad_ref,
    tok_ref, cot_ref, probs_ref, ids_ref,
    w_gu, w_down, route, send, recv, back, ret, send_far, recv_far, back_far, ret_far, raw, far_out, far_in, rows, sib_out, sib_in, rs_out, rs_in, act, fin, fin_far,
    w_sem, small_sem, a2a_send, a2a_recv, ret_send, ret_recv, a2a_far_send, a2a_far_recv, ret_far_send, ret_far_recv,
    cross_send, cross_recv,
    ag_send, ag_recv, fw_send, fw_recv, sx_send, sx_recv, rs_send, rs_recv,
):
    n_x = n_h // 2
    far = n_x // 2
    steps = far - 1
    toks, width = tok_ref.shape
    hid = gate_hbm.shape[1]
    piece = n_e * CAP // CHUNKS
    groups = n_e // CHUNKS
    block = min(16, groups)
    me_e = lax.axis_index("expert")
    me_h = lax.axis_index("hidden")
    x = me_h // 2
    core = me_h % 2

    def at(rel, other=False):
        return ((x + (rel + n_x)) % n_x) * 2 + (1 - core if other else core)

    sibling = (me_e, x * 2 + 1 - core)

    barrier = pltpu.get_barrier_semaphore()

    def greet(j, carry):
        pl.semaphore_signal(barrier, inc=1, device_id=((me_e + j) % n_e, me_h), device_id_type=MESH)
        return carry

    for d in DIRS:
        pl.semaphore_signal(barrier, inc=1, device_id=(me_e, at(d)), device_id_type=MESH)
    pl.semaphore_signal(barrier, inc=1, device_id=(me_e, at(far)), device_id_type=MESH)
    pl.semaphore_signal(barrier, inc=1, device_id=sibling, device_id_type=MESH)
    lax.fori_loop(1, n_e, greet, 0)

    small = [
        pltpu.make_async_copy(src, dst, small_sem.at[i])
        for i, (src, dst) in enumerate(
            ((ids_hbm, ids_ref), (probs_hbm, probs_ref), (tok_hbm, tok_ref), (cot_hbm, cot_ref))
        )
    ]
    loads = [
        pltpu.make_async_copy(gate_hbm.at[0], w_gu.at[pl.ds(0, hid)], w_sem.at[0]),
        pltpu.make_async_copy(up_hbm.at[0], w_gu.at[pl.ds(hid, hid)], w_sem.at[1]),
        pltpu.make_async_copy(down_hbm.at[0], w_down, w_sem.at[2]),
    ]
    for load in small + loads:
        load.start()
    for load in small:
        load.wait()

    route[...] = routing_matrix(ids_ref[...], probs_ref[...], me_e, n_e)
    halves = lambda v: [v[:, :LANES], v[:, LANES:]]

    def placed(tok, cot):
        source = jnp.concatenate(halves(tok) + halves(cot) * 3, axis=0)
        return dot(route[...], source, TN).astype(BF16)

    send[...] = placed(tok_ref[...], cot_ref[...])
    for load in loads:
        load.wait()

    pl.semaphore_wait(barrier, n_e + 3)

    n_y, n_z, turns = torus(n_e)

    def message(i, dz, p, src, dst, sems, sign):
        place = pl.ds(pl.multiple_of((i * n_z + dz) * TILE, TILE), TILE)
        y = (me_e // n_z + sign * turns[i] + n_y) % n_y
        z = (me_e % n_z + sign * dz + n_z) % n_z
        return pltpu.make_async_remote_copy(
            src_ref=src.at[place], dst_ref=dst.at[place], send_sem=sems[0].at[p], recv_sem=sems[1].at[p],
            device_id=(y * n_z + z, me_h), device_id_type=MESH,
        )

    def first(p):
        return 1 if p == 0 else p * groups

    def post(p, src, dst, sems, sign):
        per = groups // n_z

        def some(dz, carry):
            for i in range(p * per, (p + 1) * per):
                message(i, dz, p, src, dst, sems, sign).start()
            return carry

        if p == 0:
            for i in range(1, per):
                message(i, 0, p, src, dst, sems, sign).start()
        lax.fori_loop(0 if p else 1, n_z, some, 0)

    def posted(p, src, dst, sems):
        place = pl.ds(first(p) * TILE, ((p + 1) * groups - first(p)) * TILE)
        return pltpu.make_async_remote_copy(
            src_ref=src.at[place], dst_ref=dst.at[place], send_sem=sems[0].at[p], recv_sem=sems[1].at[p],
            device_id=((me_e + 1) % n_e, me_h), device_id_type=MESH,
        )

    out_way = (send, recv, (a2a_send, a2a_recv))
    home_way = (back, ret, (ret_send, ret_recv))
    out_far = (send_far, recv_far, (a2a_far_send, a2a_far_recv))
    home_far = (back_far, ret_far, (ret_far_send, ret_far_recv))

    def cross(i, src, dst):
        return pltpu.make_async_remote_copy(
            src_ref=src, dst_ref=dst, send_sem=cross_send.at[i], recv_sem=cross_recv.at[i],
            device_id=(me_e, at(far)), device_id_type=MESH,
        )

    crossing = [cross(0, tok_ref, raw.at[0]), cross(1, cot_ref, raw.at[1]), cross(2, far_out, far_in)]

    def part(p):
        return pl.ds(p * piece, piece)

    seg = block * CAP
    order = permutation(block * TILE, False)

    def arrive(p, way, rel):
        posted(p, *way).wait_recv()
        for g in range(p * groups // block, (p + 1) * groups // block):
            sorted_rows = dot(order, way[1][pl.ds(g * block * TILE, block * TILE)]).astype(BF16)
            for a in range(2):
                for half in range(2):
                    q = a * 2 + half
                    rows[a, at(rel), pl.ds(g * seg, seg), pl.ds(half * LANES, LANES)] = sorted_rows[q * seg : (q + 1) * seg]

    def ag(a, p, d, k, arriving=False):
        where = rows.at[a, at(-k * d if arriving else -(k - 1) * d), part(p)]
        i = 0 if d == 1 else 1
        return pltpu.make_async_remote_copy(
            src_ref=where, dst_ref=where, send_sem=ag_send.at[a, i, k - 1, p], recv_sem=ag_recv.at[a, i, k - 1, p],
            device_id=(me_e, at(d)), device_id_type=MESH,
        )

    def fw(a, p, rel, arriving=False):
        where = rows.at[a, at(rel, arriving), part(p)]
        return pltpu.make_async_remote_copy(
            src_ref=where, dst_ref=where, send_sem=fw_send.at[a, rel % n_x, p], recv_sem=fw_recv.at[a, rel % n_x, p],
            device_id=sibling, device_id_type=MESH,
        )

    def gather(a, p, k):
        for d in DIRS:
            if k:
                ag(a, p, d, k, True).wait_recv()
            if k < steps:
                ag(a, p, d, k + 1).start()
            if k:
                fw(a, p, -k * d).start()
        if not k:
            fw(a, p, 0).start()

    def gather_far(p):
        arrive(p, out_far, far)
        for a in range(2):
            fw(a, p, far).start()

    def cols(h):
        return pl.ds(pl.multiple_of(h * width, width), width)

    sums = {}

    def multiply(a, p, k):
        weights = w_down if a else w_gu
        for rel in (-k, k) if 0 < k < far else (k,):
            for other in (False, True):
                if other:
                    fw(a, p, rel, True).wait_recv()
                h = at(rel, other)
                term = dot(rows[a, h, part(p)], weights[:, cols(h)], NT)
                sums[a, p] = sums[a, p] + term if (a, p) in sums else term

    def own(b, p, rel, other):
        left = act[b, part(p)] if b else act[b, part(p), :hid]
        right = w_gu if b else w_down
        return dot(left, right[:, cols(at(rel, other))])

    def sx(b, p, rel):
        i = rel % n_x
        return pltpu.make_async_remote_copy(
            src_ref=sib_out.at[b, i, part(p)], dst_ref=sib_in.at[b, i, part(p)],
            send_sem=sx_send.at[b, i, p], recv_sem=sx_recv.at[b, i, p],
            device_id=sibling, device_id_type=MESH,
        )

    def exchange(b, p, k):
        for rel in (k, -k) if 0 < k < far else (k,):
            sib_out[b, rel % n_x, part(p)] = own(b, p, rel, True).astype(BF16)
            sx(b, p, rel).start()

    def forward_act(p):
        gate, up = sums[0, p][:, :hid], sums[0, p][:, hid:]
        sigma = 1.0 / (1.0 + jnp.exp(-gate))
        act[0, part(p), :hid] = (gate * sigma * up).astype(BF16)
        exchange(0, p, steps)

    def backward_act(p):
        gate, up = sums[0, p][:, :hid], sums[0, p][:, hid:]
        sigma = 1.0 / (1.0 + jnp.exp(-gate))
        act[1, part(p), :hid] = (sums[1, p] * up * sigma * (1.0 + gate * (1.0 - sigma))).astype(BF16)
        act[1, part(p), hid:] = (sums[1, p] * gate * sigma).astype(BF16)
        exchange(1, p, steps)

    def rs(b, p, d, j):
        i = 0 if d == 1 else 1
        return pltpu.make_async_remote_copy(
            src_ref=rs_out.at[b, i, j, part(p)], dst_ref=rs_in.at[b, i, j, part(p)],
            send_sem=rs_send.at[b, i, j, p], recv_sem=rs_recv.at[b, i, j, p],
            device_id=(me_e, at(d)), device_id_type=MESH,
        )

    def pair_sum(b, p, rel):
        value = own(b, p, rel, False)
        sx(b, p, rel).wait_recv()
        return value + sib_in[b, rel % n_x, part(p)].astype(F32)

    def reduce(b, p, j):
        values = [pair_sum(b, p, (steps - j) * d) for d in DIRS]
        for i, (d, value) in enumerate(zip(DIRS, values)):
            if j > 0:
                rs(b, p, d, j - 1).wait_recv()
                value = value + rs_in[b, i, j - 1, part(p)].astype(F32)
            rs_out[b, i, j, part(p)] = value.astype(BF16)
            rs(b, p, d, j).start()

    def finish(b, p):
        value = pair_sum(b, p, 0)
        for i, d in enumerate(DIRS):
            rs(b, p, d, steps - 1).wait_recv()
            value = value + rs_in[b, i, steps - 1, part(p)].astype(F32)
        fin[b, part(p)] = value.astype(BF16)

    def finish_far(p):
        for b in range(2):
            fin_far[b, part(p)] = pair_sum(b, p, far).astype(BF16)
        give_back(p, fin_far, home_far)

    inverse = permutation(block * TILE, True)

    def give_back(p, whole, way):
        for g in range(p * groups // block, (p + 1) * groups // block):
            stack = jnp.concatenate(
                [whole[b, pl.ds(g * seg, seg), pl.ds(half * LANES, LANES)] for b in (1, 0) for half in range(2)], axis=0
            )
            way[0][pl.ds(g * block * TILE, block * TILE)] = dot(inverse, stack).astype(BF16)
        post(p, *way, -1)
        if p == 0:
            way[1][pl.ds(0, TILE)] = way[0][pl.ds(0, TILE)]

    crossing[0].start()
    crossing[1].start()
    for p in range(CHUNKS):
        post(p, *out_way, 1)
    recv[pl.ds(0, TILE)] = send[pl.ds(0, TILE)]
    crossing[0].wait_recv()
    crossing[1].wait_recv()
    send_far[...] = placed(raw[0], raw[1])
    recv_far[pl.ds(0, TILE)] = send_far[pl.ds(0, TILE)]
    late = []
    for p in range(CHUNKS):
        arrive(p, out_way, 0)
        for a in range(2):
            gather(a, p, 0)
            late.append((a, p, 0))
    units = list(late)
    post(0, *out_far, 1)
    ready = []

    def start_sums(unit):
        for one in [u for u in late if u[:2] == unit]:
            late.remove(one)
            multiply(*one)
        (backward_act if unit[0] else forward_act)(unit[1])
        ready.append(unit)
        if len(ready) > 1:
            first_sums(ready[-2])

    def first_sums(unit):
        reduce(*unit, 0)
        exchange(*unit, steps - 1)

    for k in range(1, steps + 1):
        for n, (a, p, _) in enumerate(units):
            gather(a, p, k)
            if k == 1 and n == 1:
                for q in range(1, CHUNKS):
                    post(q, *out_far, 1)
            if k == steps and n > 0:
                start_sums(units[n - 1][:2])
            for unit in late[:2]:
                multiply(*unit)
            del late[:2]
            late.append((a, p, k))
            if k == steps - 1 and a == 1:
                gather_far(p)
                late += [(0, p, far), (1, p, far)]
    start_sums(units[-1][:2])
    first_sums(units[-1][:2])
    for b, p, _ in units:
        exchange(b, p, far)
    for j in range(1, steps):
        for b, p, _ in units:
            reduce(b, p, j)
            if j < steps - 1:
                exchange(b, p, steps - 1 - j)
            if j == 1:
                exchange(b, p, 0)
                if b:
                    finish_far(p)
    for b, p, _ in units:
        finish(b, p)
        if b:
            give_back(p, fin, home_way)

    def combine(way):
        total = None
        for p in range(CHUNKS):
            posted(p, *way).wait_recv()
            place = pl.ds(p * groups * TILE, groups * TILE)
            term = dot(route[:, place], way[1][place])
            total = term if total is None else total + term
        rows_of = lambda q, half: total[(q * 2 + half) * toks : (q * 2 + half + 1) * toks]
        grad = [rows_of(0, half) for half in range(2)]
        return grad, [rows_of(1, half) + rows_of(2, half) + rows_of(3, half) for half in range(2)]

    for i, pair in enumerate(combine(home_far)):
        for half in range(2):
            far_out[pl.ds(i * toks, toks), pl.ds(half * LANES, LANES)] = pair[half]
    crossing[2].start()
    near = combine(home_way)
    crossing[2].wait_recv()
    for i, (pair, out) in enumerate(zip(near, (grad_ref, mixed_ref))):
        for half in range(2):
            where = pl.ds(half * LANES, LANES)
            out[:, where] = (pair[half] + far_in[pl.ds(i * toks, toks), where]).astype(out.dtype)

    for copy in crossing:
        copy.wait_send()
    for p in range(CHUNKS):
        for way in (out_way, home_way, out_far, home_far):
            posted(p, *way).wait_send()
        for b in range(2):
            for k in range(1, steps + 1):
                for d in DIRS:
                    ag(b, p, d, k).wait_send()
                    rs(b, p, d, steps - k).wait_send()
            for rel in range(n_x):
                sx(b, p, rel).wait_send()
                fw(b, p, rel).wait_send()


def shards(tokens, probs, expert_ids, gate_weight, up_weight, down_weight, cotangent):
    n_e, n_h = lax.axis_size("expert"), lax.axis_size("hidden")
    n_x = n_h // 2
    steps = n_x // 2 - 1
    width = tokens.shape[1]
    hid, feats = gate_weight.shape[1:]
    n_rows = n_e * CAP
    dma = pltpu.SemaphoreType.DMA
    vmem = pl.BlockSpec(memory_space=pltpu.VMEM)
    hbm = pl.BlockSpec(memory_space=pltpu.HBM)
    messages = pltpu.VMEM((n_e * TILE, LANES), BF16)
    return pl.pallas_call(
        functools.partial(kernel, n_e, n_h),
        out_shape=(
            jax.ShapeDtypeStruct(tokens.shape, tokens.dtype),
            jax.ShapeDtypeStruct(tokens.shape, tokens.dtype),
        ),
        in_specs=[hbm] * 7,
        out_specs=(vmem, vmem),
        scratch_shapes=[
            pltpu.VMEM(tokens.shape, BF16),
            pltpu.VMEM(tokens.shape, BF16),
            pltpu.VMEM(probs.shape[::-1], F32),
            pltpu.VMEM(probs.shape[::-1], jnp.int32),
            pltpu.VMEM((2 * hid, feats), BF16),
            pltpu.VMEM((hid, feats), BF16),
            pltpu.VMEM((8 * tokens.shape[0], n_e * TILE), BF16),
            *[messages] * 8,
            pltpu.VMEM((2, *tokens.shape), BF16),
            pltpu.VMEM((2 * tokens.shape[0], width), F32),
            pltpu.VMEM((2 * tokens.shape[0], width), F32),
            pltpu.VMEM((2, n_h, n_rows, width), BF16),
            pltpu.VMEM((2, n_x, n_rows, width), BF16),
            pltpu.VMEM((2, n_x, n_rows, width), BF16),
            pltpu.VMEM((2, 2, steps, n_rows, width), BF16),
            pltpu.VMEM((2, 2, steps, n_rows, width), BF16),
            pltpu.VMEM((2, n_rows, 2 * hid), BF16),
            pltpu.VMEM((2, n_rows, width), BF16),
            pltpu.VMEM((2, n_rows, width), BF16),
            dma((3,)),
            dma((4,)),
            *[dma((CHUNKS,))] * 8,
            dma((3,)),
            dma((3,)),
            dma((2, 2, steps, CHUNKS)),
            dma((2, 2, steps, CHUNKS)),
            dma((2, n_x, CHUNKS)),
            dma((2, n_x, CHUNKS)),
            dma((2, n_x, CHUNKS)),
            dma((2, n_x, CHUNKS)),
            dma((2, 2, steps, CHUNKS)),
            dma((2, 2, steps, CHUNKS)),
        ],
        compiler_params=pltpu.CompilerParams(
            collective_id=0, has_side_effects=True, vmem_limit_bytes=63 * 1024 * 1024
        ),
    )(tokens, probs.T, expert_ids.T, gate_weight, up_weight, down_weight, cotangent)


def solution(mesh):
    placed = (
        P("expert", "hidden"),
        P("expert", None),
        P("expert", None),
        P("expert", "hidden", None),
        P("expert", "hidden", None),
        P("expert", "hidden", None),
        P("expert", "hidden"),
    )
    return jax.shard_map(
        shards,
        mesh=mesh,
        in_specs=placed,
        out_specs=(P("expert", "hidden"), P("expert", "hidden")),
        check_vma=False,
    )
```

```python
import functools
import math

import jax
import jax.numpy as jnp
from jax import lax
from jax.experimental import pallas as pl
from jax.experimental.pallas import tpu as pltpu
from jax.sharding import PartitionSpec as P

MESH = pl.DeviceIdType.MESH
CAP = 4
TILE = 16
LANES = 128
CHUNKS = 2
F32 = jnp.float32
BF16 = jnp.bfloat16
DIRS = (1, -1)
NT = (((1,), (1,)), ((), ()))
TN = (((0,), (0,)), ((), ()))


def dot(a, b, dims=(((1,), (0,)), ((), ()))):
    return lax.dot_general(a, b, dims, preferred_element_type=F32)


def iota(shape, axis):
    return lax.broadcasted_iota(jnp.int32, shape, axis)


def torus(n_e):
    rows = math.isqrt(n_e)
    return rows, n_e // rows, (0, 1, 7, 4, 2, 6, 3, 5) if rows == 8 else tuple(range(rows))


def routing_matrix(ids_t, probs_t, me_e, n_e):
    top, toks = ids_t.shape
    unit = (iota((top, top), 0) == iota((top, top), 1)).astype(BF16)
    turn = lambda v: dot(v.astype(BF16), unit, TN)
    ids = turn(ids_t.astype(F32)).astype(jnp.int32)
    high = probs_t.astype(BF16).astype(F32)
    middle = (probs_t - high).astype(BF16).astype(F32)
    probs = [turn(v) for v in (high, middle, probs_t - high - middle)]
    shape = (toks, n_e * TILE)
    lane = iota(shape, 1)
    n_y, n_z, order = torus(n_e)
    place = lane // TILE
    y = jnp.zeros(shape, jnp.int32)
    for i, dy in enumerate(order):
        y = jnp.where(place // n_z == i, (me_e // n_z + dy) % n_y, y)
    expert = y * n_z + (place % n_z + me_e) % n_z
    part = (lane % TILE) // CAP
    slot = (lane % CAP).astype(F32)
    member = jnp.zeros(shape, F32)
    weights = [jnp.zeros(shape, F32)] * 3
    for k in range(top):
        same = ids[:, k : k + 1] == expert
        member = jnp.where(same, 1.0, member)
        weights = [jnp.where(same, v[:, k : k + 1], w) for v, w in zip(probs, weights)]
    before = (iota((toks, toks), 1) < iota((toks, toks), 0)).astype(BF16)
    count = dot(before, member.astype(BF16))
    pick = jnp.where(count == slot, member, 0.0)
    blocks = []
    for q, value in enumerate([pick] + [pick * w for w in weights]):
        for half in range(2):
            here = part == (0 if q == 0 else 2) + half
            blocks.append(jnp.where(here, value, 0.0).astype(BF16))
    return jnp.concatenate(blocks, axis=0)


def permutation(size, inverse):
    seg = size // 4
    o = iota((size, size), 1 if inverse else 0)
    i = iota((size, size), 0 if inverse else 1)
    rest = o % seg
    return (i == (rest // CAP) * TILE + (o // seg) * CAP + rest % CAP).astype(BF16)


def kernel(
    n_e, n_h, tok_hbm, probs_hbm, ids_hbm, gate_hbm, up_hbm, down_hbm, cot_hbm,
    mixed_ref, grad_ref,
    tok_ref, cot_ref, probs_ref, ids_ref,
    w_gu, w_down, route, send, recv, back, ret, send_far, recv_far, back_far, ret_far, raw, far_out, far_in, rows, sib_out, sib_in, rs_out, rs_in, act, fin, fin_far,
    w_sem, small_sem, a2a_send, a2a_recv, ret_send, ret_recv, a2a_far_send, a2a_far_recv, ret_far_send, ret_far_recv,
    cross_send, cross_recv,
    ag_send, ag_recv, fw_send, fw_recv, sx_send, sx_recv, rs_send, rs_recv,
):
    n_x = n_h // 2
    far = n_x // 2
    steps = far - 1
    toks, width = tok_ref.shape
    hid = gate_hbm.shape[1]
    piece = n_e * CAP // CHUNKS
    groups = n_e // CHUNKS
    block = min(16, groups)
    me_e = lax.axis_index("expert")
    me_h = lax.axis_index("hidden")
    x = me_h // 2
    core = me_h % 2

    def at(rel, other=False):
        return ((x + (rel + n_x)) % n_x) * 2 + (1 - core if other else core)

    sibling = (me_e, x * 2 + 1 - core)

    barrier = pltpu.get_barrier_semaphore()

    def greet(j, carry):
        pl.semaphore_signal(barrier, inc=1, device_id=((me_e + j) % n_e, me_h), device_id_type=MESH)
        return carry

    for d in DIRS:
        pl.semaphore_signal(barrier, inc=1, device_id=(me_e, at(d)), device_id_type=MESH)
    pl.semaphore_signal(barrier, inc=1, device_id=(me_e, at(far)), device_id_type=MESH)
    pl.semaphore_signal(barrier, inc=1, device_id=sibling, device_id_type=MESH)
    lax.fori_loop(1, n_e, greet, 0)

    small = [
        pltpu.make_async_copy(src, dst, small_sem.at[i])
        for i, (src, dst) in enumerate(
            ((ids_hbm, ids_ref), (probs_hbm, probs_ref), (tok_hbm, tok_ref), (cot_hbm, cot_ref))
        )
    ]
    loads = [
        pltpu.make_async_copy(gate_hbm.at[0], w_gu.at[pl.ds(0, hid)], w_sem.at[0]),
        pltpu.make_async_copy(up_hbm.at[0], w_gu.at[pl.ds(hid, hid)], w_sem.at[1]),
        pltpu.make_async_copy(down_hbm.at[0], w_down, w_sem.at[2]),
    ]
    for load in small + loads:
        load.start()
    for load in small:
        load.wait()

    route[...] = routing_matrix(ids_ref[...], probs_ref[...], me_e, n_e)
    halves = lambda v: [v[:, :LANES], v[:, LANES:]]

    def placed(tok, cot):
        source = jnp.concatenate(halves(tok) + halves(cot) * 3, axis=0)
        return dot(route[...], source, TN).astype(BF16)

    send[...] = placed(tok_ref[...], cot_ref[...])
    for load in loads:
        load.wait()

    pl.semaphore_wait(barrier, n_e + 3)

    n_y, n_z, turns = torus(n_e)

    def message(i, dz, p, src, dst, sems, sign):
        place = pl.ds(pl.multiple_of((i * n_z + dz) * TILE, TILE), TILE)
        y = (me_e // n_z + sign * turns[i] + n_y) % n_y
        z = (me_e % n_z + sign * dz + n_z) % n_z
        return pltpu.make_async_remote_copy(
            src_ref=src.at[place], dst_ref=dst.at[place], send_sem=sems[0].at[p], recv_sem=sems[1].at[p],
            device_id=(y * n_z + z, me_h), device_id_type=MESH,
        )

    def first(p):
        return 1 if p == 0 else p * groups

    def post(p, src, dst, sems, sign):
        per = groups // n_z

        def some(turn, carry):
            near = n_z - 1 - turn
            dz = (near % 2 * ((near + 1) // 2) + (1 - near % 2) * (n_z - near // 2)) % n_z
            for i in reversed(range(p * per, (p + 1) * per)):
                message(i, dz, p, src, dst, sems, sign).start()
            return carry

        if p == 0:
            for i in range(1, per):
                message(i, 0, p, src, dst, sems, sign).start()
        lax.fori_loop(0, n_z if p else n_z - 1, some, 0)

    def posted(p, src, dst, sems):
        place = pl.ds(first(p) * TILE, ((p + 1) * groups - first(p)) * TILE)
        return pltpu.make_async_remote_copy(
            src_ref=src.at[place], dst_ref=dst.at[place], send_sem=sems[0].at[p], recv_sem=sems[1].at[p],
            device_id=((me_e + 1) % n_e, me_h), device_id_type=MESH,
        )

    out_way = (send, recv, (a2a_send, a2a_recv))
    home_way = (back, ret, (ret_send, ret_recv))
    out_far = (send_far, recv_far, (a2a_far_send, a2a_far_recv))
    home_far = (back_far, ret_far, (ret_far_send, ret_far_recv))

    def cross(i, src, dst):
        return pltpu.make_async_remote_copy(
            src_ref=src, dst_ref=dst, send_sem=cross_send.at[i], recv_sem=cross_recv.at[i],
            device_id=(me_e, at(far)), device_id_type=MESH,
        )

    crossing = [cross(0, tok_ref, raw.at[0]), cross(1, cot_ref, raw.at[1]), cross(2, far_out, far_in)]

    def part(p):
        return pl.ds(p * piece, piece)

    seg = block * CAP
    order = permutation(block * TILE, False)

    def arrive(p, way, rel):
        posted(p, *way).wait_recv()
        for g in range(p * groups // block, (p + 1) * groups // block):
            sorted_rows = dot(order, way[1][pl.ds(g * block * TILE, block * TILE)]).astype(BF16)
            for a in range(2):
                for half in range(2):
                    q = a * 2 + half
                    rows[a, at(rel), pl.ds(g * seg, seg), pl.ds(half * LANES, LANES)] = sorted_rows[q * seg : (q + 1) * seg]

    def ag(a, p, d, k, arriving=False):
        where = rows.at[a, at(-k * d if arriving else -(k - 1) * d), part(p)]
        i = 0 if d == 1 else 1
        return pltpu.make_async_remote_copy(
            src_ref=where, dst_ref=where, send_sem=ag_send.at[a, i, k - 1, p], recv_sem=ag_recv.at[a, i, k - 1, p],
            device_id=(me_e, at(d)), device_id_type=MESH,
        )

    def fw(a, p, rel, arriving=False):
        where = rows.at[a, at(rel, arriving), part(p)]
        return pltpu.make_async_remote_copy(
            src_ref=where, dst_ref=where, send_sem=fw_send.at[a, rel % n_x, p], recv_sem=fw_recv.at[a, rel % n_x, p],
            device_id=sibling, device_id_type=MESH,
        )

    def gather(a, p, k):
        for d in DIRS:
            if k:
                ag(a, p, d, k, True).wait_recv()
            if k < steps:
                ag(a, p, d, k + 1).start()
        for rel in (-k, k) if k else (0,):
            fw(a, p, rel).start()

    def gather_far(p):
        arrive(p, out_far, far)
        for a in range(2):
            fw(a, p, far).start()

    def cols(h):
        return pl.ds(pl.multiple_of(h * width, width), width)

    sums = {}

    def multiply(a, p, k):
        weights = w_down if a else w_gu
        for rel in (-k, k) if 0 < k < far else (k,):
            for other in (False, True):
                if other:
                    fw(a, p, rel, True).wait_recv()
                h = at(rel, other)
                term = dot(rows[a, h, part(p)], weights[:, cols(h)], NT)
                sums[a, p] = sums[a, p] + term if (a, p) in sums else term

    def own(b, p, rel, other):
        left = act[b, part(p)] if b else act[b, part(p), :hid]
        right = w_gu if b else w_down
        return dot(left, right[:, cols(at(rel, other))])

    def sx(b, p, rel):
        i = rel % n_x
        return pltpu.make_async_remote_copy(
            src_ref=sib_out.at[b, i, part(p)], dst_ref=sib_in.at[b, i, part(p)],
            send_sem=sx_send.at[b, i, p], recv_sem=sx_recv.at[b, i, p],
            device_id=sibling, device_id_type=MESH,
        )

    def exchange(b, p, k):
        for rel in (k, -k) if 0 < k < far else (k,):
            sib_out[b, rel % n_x, part(p)] = own(b, p, rel, True).astype(BF16)
            sx(b, p, rel).start()

    def forward_act(p):
        gate, up = sums[0, p][:, :hid], sums[0, p][:, hid:]
        sigma = 1.0 / (1.0 + jnp.exp(-gate))
        act[0, part(p), :hid] = (gate * sigma * up).astype(BF16)
        exchange(0, p, steps)

    def backward_act(p):
        gate, up = sums[0, p][:, :hid], sums[0, p][:, hid:]
        sigma = 1.0 / (1.0 + jnp.exp(-gate))
        act[1, part(p), :hid] = (sums[1, p] * up * sigma * (1.0 + gate * (1.0 - sigma))).astype(BF16)
        act[1, part(p), hid:] = (sums[1, p] * gate * sigma).astype(BF16)
        exchange(1, p, steps)

    def rs(b, p, d, j):
        i = 0 if d == 1 else 1
        return pltpu.make_async_remote_copy(
            src_ref=rs_out.at[b, i, j, part(p)], dst_ref=rs_in.at[b, i, j, part(p)],
            send_sem=rs_send.at[b, i, j, p], recv_sem=rs_recv.at[b, i, j, p],
            device_id=(me_e, at(d)), device_id_type=MESH,
        )

    def pair_sum(b, p, rel):
        value = own(b, p, rel, False)
        sx(b, p, rel).wait_recv()
        return value + sib_in[b, rel % n_x, part(p)].astype(F32)

    def reduce(b, p, j):
        values = [pair_sum(b, p, (steps - j) * d) for d in DIRS]
        for i, (d, value) in enumerate(zip(DIRS, values)):
            if j > 0:
                rs(b, p, d, j - 1).wait_recv()
                value = value + rs_in[b, i, j - 1, part(p)].astype(F32)
            rs_out[b, i, j, part(p)] = value.astype(BF16)
            rs(b, p, d, j).start()

    def finish(b, p):
        value = pair_sum(b, p, 0)
        for i, d in enumerate(DIRS):
            rs(b, p, d, steps - 1).wait_recv()
            value = value + rs_in[b, i, steps - 1, part(p)].astype(F32)
        fin[b, part(p)] = value.astype(BF16)

    def finish_far(p):
        for b in range(2):
            fin_far[b, part(p)] = pair_sum(b, p, far).astype(BF16)
        give_back(p, fin_far, home_far)

    inverse = permutation(block * TILE, True)

    def give_back(p, whole, way):
        for g in range(p * groups // block, (p + 1) * groups // block):
            stack = jnp.concatenate(
                [whole[b, pl.ds(g * seg, seg), pl.ds(half * LANES, LANES)] for b in (1, 0) for half in range(2)], axis=0
            )
            way[0][pl.ds(g * block * TILE, block * TILE)] = dot(inverse, stack).astype(BF16)
        post(p, *way, -1)
        if p == 0:
            way[1][pl.ds(0, TILE)] = way[0][pl.ds(0, TILE)]

    crossing[0].start()
    crossing[1].start()
    for p in range(CHUNKS):
        post(p, *out_way, 1)
    recv[pl.ds(0, TILE)] = send[pl.ds(0, TILE)]
    crossing[0].wait_recv()
    crossing[1].wait_recv()
    send_far[...] = placed(raw[0], raw[1])
    recv_far[pl.ds(0, TILE)] = send_far[pl.ds(0, TILE)]
    late = []
    for p in range(CHUNKS):
        arrive(p, out_way, 0)
        for a in range(2):
            gather(a, p, 0)
            late.append((a, p, 0))
    units = list(late)
    post(0, *out_far, 1)
    ready = []

    def start_sums(unit):
        for one in [u for u in late if u[:2] == unit]:
            late.remove(one)
            multiply(*one)
        (backward_act if unit[0] else forward_act)(unit[1])
        ready.append(unit)
        if len(ready) > 1:
            first_sums(ready[-2])

    def first_sums(unit):
        reduce(*unit, 0)
        exchange(*unit, steps - 1)

    for k in range(1, steps + 1):
        for n, (a, p, _) in enumerate(units):
            gather(a, p, k)
            if k == 1 and n == 1:
                for q in range(1, CHUNKS):
                    post(q, *out_far, 1)
            if k == steps and n > 0:
                start_sums(units[n - 1][:2])
            for unit in late[:2]:
                multiply(*unit)
            del late[:2]
            late.append((a, p, k))
            if k == steps - 1 and a == 1:
                gather_far(p)
                late += [(0, p, far), (1, p, far)]
    start_sums(units[-1][:2])
    first_sums(units[-1][:2])
    for b, p, _ in units:
        exchange(b, p, far)
    for j in range(1, steps):
        for b, p, _ in units:
            reduce(b, p, j)
            if j < steps - 1:
                exchange(b, p, steps - 1 - j)
            if j == 1:
                exchange(b, p, 0)
                if b:
                    finish_far(p)
    for b, p, _ in units:
        finish(b, p)
        if b:
            give_back(p, fin, home_way)

    def combine(way):
        total = None
        for p in range(CHUNKS):
            posted(p, *way).wait_recv()
            place = pl.ds(p * groups * TILE, groups * TILE)
            term = dot(route[:, place], way[1][place])
            total = term if total is None else total + term
        rows_of = lambda q, half: total[(q * 2 + half) * toks : (q * 2 + half + 1) * toks]
        grad = [rows_of(0, half) for half in range(2)]
        return grad, [rows_of(1, half) + rows_of(2, half) + rows_of(3, half) for half in range(2)]

    for i, pair in enumerate(combine(home_far)):
        for half in range(2):
            far_out[pl.ds(i * toks, toks), pl.ds(half * LANES, LANES)] = pair[half]
    crossing[2].start()
    near = combine(home_way)
    crossing[2].wait_recv()
    for i, (pair, out) in enumerate(zip(near, (grad_ref, mixed_ref))):
        for half in range(2):
            where = pl.ds(half * LANES, LANES)
            out[:, where] = (pair[half] + far_in[pl.ds(i * toks, toks), where]).astype(out.dtype)

    for copy in crossing:
        copy.wait_send()
    for p in range(CHUNKS):
        for way in (out_way, home_way, out_far, home_far):
            posted(p, *way).wait_send()
        for b in range(2):
            for k in range(1, steps + 1):
                for d in DIRS:
                    ag(b, p, d, k).wait_send()
                    rs(b, p, d, steps - k).wait_send()
            for rel in range(n_x):
                sx(b, p, rel).wait_send()
                fw(b, p, rel).wait_send()


def shards(tokens, probs, expert_ids, gate_weight, up_weight, down_weight, cotangent):
    n_e, n_h = lax.axis_size("expert"), lax.axis_size("hidden")
    n_x = n_h // 2
    steps = n_x // 2 - 1
    width = tokens.shape[1]
    hid, feats = gate_weight.shape[1:]
    n_rows = n_e * CAP
    dma = pltpu.SemaphoreType.DMA
    vmem = pl.BlockSpec(memory_space=pltpu.VMEM)
    hbm = pl.BlockSpec(memory_space=pltpu.HBM)
    messages = pltpu.VMEM((n_e * TILE, LANES), BF16)
    return pl.pallas_call(
        functools.partial(kernel, n_e, n_h),
        out_shape=(
            jax.ShapeDtypeStruct(tokens.shape, tokens.dtype),
            jax.ShapeDtypeStruct(tokens.shape, tokens.dtype),
        ),
        in_specs=[hbm] * 7,
        out_specs=(vmem, vmem),
        scratch_shapes=[
            pltpu.VMEM(tokens.shape, BF16),
            pltpu.VMEM(tokens.shape, BF16),
            pltpu.VMEM(probs.shape[::-1], F32),
            pltpu.VMEM(probs.shape[::-1], jnp.int32),
            pltpu.VMEM((2 * hid, feats), BF16),
            pltpu.VMEM((hid, feats), BF16),
            pltpu.VMEM((8 * tokens.shape[0], n_e * TILE), BF16),
            *[messages] * 8,
            pltpu.VMEM((2, *tokens.shape), BF16),
            pltpu.VMEM((2 * tokens.shape[0], width), F32),
            pltpu.VMEM((2 * tokens.shape[0], width), F32),
            pltpu.VMEM((2, n_h, n_rows, width), BF16),
            pltpu.VMEM((2, n_x, n_rows, width), BF16),
            pltpu.VMEM((2, n_x, n_rows, width), BF16),
            pltpu.VMEM((2, 2, steps, n_rows, width), BF16),
            pltpu.VMEM((2, 2, steps, n_rows, width), BF16),
            pltpu.VMEM((2, n_rows, 2 * hid), BF16),
            pltpu.VMEM((2, n_rows, width), BF16),
            pltpu.VMEM((2, n_rows, width), BF16),
            dma((3,)),
            dma((4,)),
            *[dma((CHUNKS,))] * 8,
            dma((3,)),
            dma((3,)),
            dma((2, 2, steps, CHUNKS)),
            dma((2, 2, steps, CHUNKS)),
            dma((2, n_x, CHUNKS)),
            dma((2, n_x, CHUNKS)),
            dma((2, n_x, CHUNKS)),
            dma((2, n_x, CHUNKS)),
            dma((2, 2, steps, CHUNKS)),
            dma((2, 2, steps, CHUNKS)),
        ],
        compiler_params=pltpu.CompilerParams(
            collective_id=0, has_side_effects=True, vmem_limit_bytes=63 * 1024 * 1024
        ),
    )(tokens, probs.T, expert_ids.T, gate_weight, up_weight, down_weight, cotangent)


def solution(mesh):
    placed = (
        P("expert", "hidden"),
        P("expert", None),
        P("expert", None),
        P("expert", "hidden", None),
        P("expert", "hidden", None),
        P("expert", "hidden", None),
        P("expert", "hidden"),
    )
    return jax.shard_map(
        shards,
        mesh=mesh,
        in_specs=placed,
        out_specs=(P("expert", "hidden"), P("expert", "hidden")),
        check_vma=False,
    )
```
